512 devices in a mesh: section: 8 (over z_lo), seq: 8 (over z_hi, x), tensor: 8 (over y, core).
Axes of the slice: x: 4, y: 4, z: 16 (z_hi: 2, z_lo: 8; z = z_hi * 8 + z_lo), core: 2. Of those that a mesh axis runs over, the one named last changes fastest.
Arguments:
- acts: bfloat16 [8, 512, 8192], P('section', 'seq', 'tensor'), may hold values from -6 to 6
- incoming: bfloat16 [8, 512, 8192], P('section', 'seq', 'tensor'), may hold values from -6 to 6
- rotation: bfloat16 [8192, 8192], P('tensor', 'seq'), may hold values from -0.0625 to 0.0625
- q_weight: bfloat16 [8, 8192, 8192], P('section', 'seq', 'tensor'), may hold values from -0.0625 to 0.0625
- w_exponents: int32 [8, 8192], P('section', 'tensor'), may hold values from -13 to -9
Outputs:
- r1_grad: float32 [8192, 8192], P(('tensor', 'section'), 'seq')
- grad_rotated: bfloat16 [8, 512, 8192], P('section', 'tensor', 'seq')
The draws below stay inside these ranges and needn't reach their ends.
All inputs are finite; a program needn't handle non-finite values.
Results may differ from the reference program's by a relative error of at most 0.027.
Values may be sent and summed in bfloat16 or wider, within the bound.
A program may use at most 64 MiB of HBM per device.

```python
import jax
import jax.numpy as jnp
from jax import lax

D = 8192
E = 8192
TOKENS = 512
SECTIONS = 8
N_TENSOR = 8


def touch_ends(values, own_key, low, largest):
    longest = values.shape.index(max(values.shape))
    spots = []
    for shift in (0, 1):
        where = [jax.random.randint(jax.random.fold_in(own_key, axis), (), 0, length) for axis, length in enumerate(values.shape)]
        where[longest] = (where[longest] + shift) % values.shape[longest]
        spots.append(tuple(where))
    return values.at[spots[0]].set(low).at[spots[1]].set(largest)


def steps_of(stream_key, dims, shards, least, largest):
    factor_of, own = 1.0, jax.random.fold_in(stream_key, 6)
    for position, blocks in shards:
        heights = jnp.exp(jax.random.uniform(jax.random.fold_in(own, position), (blocks,), jnp.float32, least / len(shards), largest / len(shards)))
        factor_of = factor_of * jnp.repeat(heights, dims[position] // blocks).reshape([-1 if axis == position else 1 for axis in range(len(dims))])
    return factor_of


def bell_draw(rng, dims, deviation, limit, pieces=(), dtype=jnp.bfloat16):
    loudness = steps_of(rng, dims, pieces, -0.22, 0.18) if pieces else 1.0
    result = jax.random.normal(rng, dims, jnp.float32) * deviation * loudness
    return jnp.minimum(jnp.maximum(result, -limit), limit).astype(dtype)


def setup_inputs(seed: int = 0) -> dict:
    key_list = jax.random.split(jax.random.key(seed), 6)
    return {
        "acts": bell_draw(key_list[0], (SECTIONS, TOKENS, D), 1.0, 6.0, ((0, 8), (1, 8), (2, 8))),
        "incoming": bell_draw(key_list[1], (SECTIONS, TOKENS, E), 1.0, 6.0, ((0, 8), (1, 8), (2, 8))),
        "rotation": bell_draw(key_list[2], (D, D), D ** -0.5, 0.0625, ((0, 8), (1, 8))),
        "q_weight": bell_draw(key_list[3], (SECTIONS, D, E), D ** -0.5, 0.0625, ((0, 8), (1, 8), (2, 8))),
        "w_exponents": touch_ends(jax.random.randint(key_list[4], (SECTIONS, E), -13, -8), jax.random.fold_in(key_list[4], 1), -13, (-8) - 1).astype(jnp.int32),
    }


act_clip = 0.5


def rounded(value):
    return lax.optimization_barrier(value.astype(jnp.bfloat16)).astype(jnp.float32)


def section_work(acts_one, upstream, weight, expos, rotation):
    tok = acts_one.shape[0]
    width = D // N_TENSOR
    rotated = jnp.zeros((tok, D), jnp.float32)
    for block in range(N_TENSOR):
        part = jnp.dot(acts_one[:, block * width:(block + 1) * width], rotation[block * width:(block + 1) * width, :], preferred_element_type=jnp.float32)
        rotated = rotated + rounded(part)
    peaks = jnp.max(jnp.abs(rotated), axis=1)
    clip = act_clip * (peaks + 1e-6)
    scale = 127.0 * jnp.exp2(expos.astype(jnp.float32))
    quantized = (scale[None, :] * jnp.tanh(weight.astype(jnp.float32) / scale[None, :])).astype(jnp.bfloat16)
    eblock = E // N_TENSOR
    back = jnp.zeros((tok, D), jnp.float32)
    for block in range(N_TENSOR):
        part = jnp.dot(upstream[:, block * eblock:(block + 1) * eblock], quantized[:, block * eblock:(block + 1) * eblock].T, preferred_element_type=jnp.float32)
        back = back + rounded(part)
    ratio = jnp.tanh(rotated / clip[:, None])
    grad_rot = (back * (1.0 - ratio * ratio)).astype(jnp.bfloat16)
    partial_grad = rounded(jnp.dot(acts_one.T, grad_rot, preferred_element_type=jnp.float32))
    return grad_rot, partial_grad


def reference(acts, incoming, rotation, q_weight, w_exponents):
    following = jnp.concatenate([incoming[1:], incoming[-1:]], axis=0)

    def step(total, items):
        acts_one, upstream, weight, expos = items
        grad_rot, partial_grad = section_work(acts_one, upstream, weight, expos, rotation)
        return total + partial_grad, grad_rot

    total, grads = lax.scan(step, jnp.zeros((D, D), jnp.float32), (acts, following, q_weight, w_exponents))
    return total, grads
```

```python
import jax
import jax.numpy as jnp
from jax import lax
from jax.experimental import pallas as pl
from jax.experimental.pallas import tpu as pltpu
from jax.sharding import PartitionSpec as P

F32, BF16 = jnp.float32, jnp.bfloat16
ACT_CLIP = 0.5
NX, NY = 4, 4
TOK = 64
WIDE = 1024
SHARD = 128
PARTS = 2
PCOL = WIDE // PARTS
TILE = 256


def kernel(
    acts, incoming, rotation, weight, expos,
    total, grad_out,
    tok_a, tok_u, rot_v, w_v, quant, acts_t,
    prod_a, prod_u, core_a, core_u, send_a, send_u, recv_a, recv_u,
    own_a, own_u, peak_own, peak_recv, gate, grads,
    right_send, right_recv, left_send, left_recv,
    local_sem, gather_a_s, gather_a_r, gather_u_s, gather_u_r,
    core_s, core_r, ring_s, ring_r, peak_s, peak_r, grad_s, grad_r,
    right_s, right_r, left_s, left_r,
):
    n_sec = lax.axis_size("section")
    s = lax.axis_index("section")
    q = lax.axis_index("seq")
    t = lax.axis_index("tensor")
    zh, x = q // NX, q % NX
    y, c = t // 2, t % 2
    last = n_sec - 1

    def at_x(k):
        return (s, zh * NX + (x + k) % NX, t)

    def at_y(k):
        return (s, q, ((y + k) % NY) * 2 + c)

    far = (s, (1 - zh) * NX + x, t)
    mate = (s, q, y * 2 + 1 - c)
    up, down = (s + 1, q, t), (s - 1, q, t)

    def signal(device):
        pl.semaphore_signal(barrier, inc=1, device_id=device, device_id_type=pl.DeviceIdType.MESH)

    def send(src, dst, ssem, rsem, device):
        return pltpu.make_async_remote_copy(
            src_ref=src, dst_ref=dst, send_sem=ssem, recv_sem=rsem,
            device_id=device, device_id_type=pl.DeviceIdType.MESH,
        )

    def rows(block, size=TOK):
        return pl.ds(pl.multiple_of(block * size, size), size)

    load_rot = pltpu.make_async_copy(rotation, rot_v, local_sem.at[0])
    load_w = pltpu.make_async_copy(weight.at[0], w_v, local_sem.at[1])
    load_a = pltpu.make_async_copy(acts.at[0], tok_a.at[rows(q)], local_sem.at[2])
    load_u = pltpu.make_async_copy(incoming.at[0], tok_u.at[rows(q)], local_sem.at[3])
    load_a.start()
    load_w.start()
    load_rot.start()

    @pl.when(s == last)
    def _():
        load_u.start()

    barrier = pltpu.get_barrier_semaphore()
    for k in (1, 2, 3):
        signal(at_x(k))
        signal(at_y(k))
    signal(far)
    signal(mate)

    @pl.when(s < last)
    def _():
        signal(up)

    @pl.when(s > 0)
    def _():
        signal(down)

    pl.semaphore_wait(
        barrier, 8 + jnp.where(s < last, 1, 0) + jnp.where(s > 0, 1, 0)
    )

    mine, other = rows(q), rows((1 - zh) * NX + x)
    a_far = send(acts.at[0], tok_a.at[mine], gather_a_s.at[3], gather_a_r.at[3], far)
    a_near = [
        send(acts.at[0], tok_a.at[mine], gather_a_s.at[k - 1], gather_a_r.at[k - 1], at_x(k))
        for k in (1, 2, 3)
    ]
    a_pass = [
        send(tok_a.at[other], tok_a.at[other], gather_a_s.at[k + 3], gather_a_r.at[k + 3], at_x(k))
        for k in (1, 2, 3)
    ]
    u_shift = send(incoming.at[0], tok_u.at[mine], gather_u_s.at[7], gather_u_r.at[7], down)
    u_far = send(tok_u.at[mine], tok_u.at[mine], gather_u_s.at[3], gather_u_r.at[3], far)
    u_near = [
        send(tok_u.at[mine], tok_u.at[mine], gather_u_s.at[k - 1], gather_u_r.at[k - 1], at_x(k))
        for k in (1, 2, 3)
    ]
    u_pass = [
        send(tok_u.at[other], tok_u.at[other], gather_u_s.at[k + 3], gather_u_r.at[k + 3], at_x(k))
        for k in (1, 2, 3)
    ]

    @pl.when(s > 0)
    def _():
        u_shift.start()

    a_far.start()
    for copy in a_near:
        copy.start()

    @pl.when(s < last)
    def _():
        u_shift.wait_recv()

    @pl.when(s == last)
    def _():
        load_u.wait()

    u_far.start()
    for copy in u_near:
        copy.start()

    load_w.wait()
    scale = 127.0 * jnp.exp2(expos[...].astype(F32))
    inverse = 1.0 / scale

    def quantize(i, carry):
        r = rows(i, 64)
        quant[r] = (scale * jnp.tanh(w_v[r].astype(F32) * inverse)).astype(BF16)
        return carry

    lax.fori_loop(0, WIDE // 64, quantize, 0)
    load_rot.wait()
    load_a.wait()

    def project(half, tok, mat, flip, prod, core_in, base):
        r = pl.ds(pl.multiple_of(half * (NX * TOK), NX * TOK), NX * TOK)

        def tile(n, carry):
            cols = pl.ds(pl.multiple_of(n * TILE, TILE), TILE)
            if flip:
                part = lax.dot_general(
                    tok[r], mat[cols], (((1,), (1,)), ((), ())), preferred_element_type=F32
                )
            else:
                part = jnp.dot(tok[r], mat[:, cols], preferred_element_type=F32)
            prod[r, cols] = part.astype(BF16)
            return carry

        lax.fori_loop(0, WIDE // TILE, tile, 0)
        copies = []
        for j in (0, 1):
            chip = half * 2 + j
            copy = send(
                prod.at[rows(chip * 2 + 1 - c)], core_in.at[chip],
                core_s.at[base + j], core_r.at[base + j], mate,
            )
            copy.start()
            copies.append(copy)
        return copies

    def scatter(half, copies, prod, core_in, out, landing, own, base):
        for j in (0, 1):
            chip = half * 2 + j
            copies[j].wait_recv()
            both = prod[rows(chip * 2 + c)].astype(F32) + core_in[chip].astype(F32)

            @pl.when(chip == y)
            def _():
                own[...] = both

            @pl.when(chip != y)
            def _():
                k = (chip - y + NY) % NY - 1
                out[chip] = both.astype(BF16)
                send(
                    out.at[chip], landing.at[k], ring_s.at[base + k], ring_r.at[base + k],
                    (s, q, chip * 2 + c),
                ).start()

    def collect(out, landing, own, base):
        value = own[...]
        for k in range(3):
            send(out.at[0], landing.at[k], ring_s.at[base + k], ring_r.at[base + k], at_y(k + 1)).wait_recv()
            value = value + landing[k].astype(F32)
        return value

    near_half, far_half = zh, 1 - zh
    for copy in a_near:
        copy.wait_recv()
    ca_near = project(near_half, tok_a, rot_v, False, prod_a, core_a, 0)
    for copy in u_near:
        copy.wait_recv()
    cu_near = project(near_half, tok_u, quant, True, prod_u, core_u, 4)
    scatter(near_half, ca_near, prod_a, core_a, send_a, recv_a, own_a, 0)

    a_far.wait_recv()
    for copy in a_pass:
        copy.start()
    scatter(near_half, cu_near, prod_u, core_u, send_u, recv_u, own_u, 3)
    for copy in a_pass:
        copy.wait_recv()
    ca_far = project(far_half, tok_a, rot_v, False, prod_a, core_a, 2)
    scatter(far_half, ca_far, prod_a, core_a, send_a, recv_a, own_a, 0)

    u_far.wait_recv()
    for copy in u_pass:
        copy.start()

    rotated = collect(send_a, recv_a, own_a, 0)
    own_a[...] = rotated
    diagonal = lax.broadcasted_iota(jnp.int32, (TOK, 128), 0) == lax.broadcasted_iota(
        jnp.int32, (TOK, 128), 1
    )
    peak = jnp.max(jnp.abs(rotated), axis=1, keepdims=True)
    line = jnp.max(jnp.where(diagonal, peak, 0.0), axis=0, keepdims=True)
    peak_own[0] = jnp.broadcast_to(line, (8, 128))
    peak_x = [
        send(peak_own.at[0], peak_recv.at[k - 1], peak_s.at[k - 1], peak_r.at[k - 1], at_x(k))
        for k in (1, 2, 3)
    ]
    peak_z = send(peak_own.at[1], peak_recv.at[3], peak_s.at[3], peak_r.at[3], far)
    for copy in peak_x:
        copy.start()

    def turn(i, carry):
        r = pl.ds(pl.multiple_of(i * 128, 128), 128)
        acts_t[r] = tok_a[:, r].T
        return carry

    for copy in peak_x:
        copy.wait_recv()
    peak_own[1] = jnp.maximum(
        jnp.maximum(peak_own[0], peak_recv[0]), jnp.maximum(peak_recv[1], peak_recv[2])
    )
    peak_z.start()
    lax.fori_loop(0, WIDE // 128, turn, 0)
    for copy in u_pass:
        copy.wait_recv()
    cu_far = project(far_half, tok_u, quant, True, prod_u, core_u, 6)
    peak_z.wait_recv()
    line = jnp.maximum(peak_own[1], peak_recv[3])[0:1]
    peak = jnp.max(jnp.where(diagonal, line, 0.0), axis=1, keepdims=True)
    clip = ACT_CLIP * (peak + 1e-06)
    ratio = jnp.tanh(own_a[...] * (1.0 / clip))
    gate[...] = 1.0 - ratio * ratio
    scatter(far_half, cu_far, prod_u, core_u, send_u, recv_u, own_u, 3)
    back = collect(send_u, recv_u, own_u, 3)
    grad = (back * gate[...]).astype(BF16)
    grad_out[0] = grad
    grads[rows(t)] = grad

    g_y = [
        send(grads.at[rows(t)], grads.at[rows(t)], grad_s.at[k - 1], grad_r.at[k - 1], at_y(k))
        for k in (1, 2, 3)
    ]
    g_core = send(grads.at[rows(t)], grads.at[rows(t)], grad_s.at[3], grad_r.at[3], mate)
    g_pass = []
    for k in (1, 2, 3):
        block = rows(((y - k + NY) % NY) * 2 + c)
        g_pass.append(
            send(grads.at[block], grads.at[block], grad_s.at[3 + k], grad_r.at[3 + k], mate)
        )
    for copy in g_y:
        copy.start()
    g_core.start()
    for arrived, onward in zip(g_y, g_pass):
        arrived.wait_recv()
        onward.start()
    g_core.wait_recv()
    for copy in g_pass:
        copy.wait_recv()

    def partial(shard, p):
        return jnp.dot(
            acts_t[rows(shard, SHARD)], grads[:, p * PCOL : (p + 1) * PCOL],
            preferred_element_type=F32,
        )

    def hop(shard, p, out, landing, ssem, rsem, device):
        return send(
            out.at[shard, p], landing.at[shard, p], ssem.at[shard, p], rsem.at[shard, p], device
        )

    def step(tau, carry):
        for p in range(PARTS):

            @pl.when(tau >= s)
            def _():
                shard = last - (tau - s)
                value = partial(shard, p)
                copy = hop(shard, p, right_send, right_recv, right_s, right_r, up)

                @pl.when(s > 0)
                def _():
                    copy.wait_recv()
                    right_send[shard, p] = (value + right_recv[shard, p].astype(F32)).astype(BF16)

                @pl.when(s == 0)
                def _():
                    right_send[shard, p] = value.astype(BF16)

                copy.start()

            @pl.when(tau >= last - s)
            def _():
                shard = tau - (last - s)
                value = partial(shard, p)
                copy = hop(shard, p, left_send, left_recv, left_s, left_r, down)

                @pl.when(s < last)
                def _():
                    copy.wait_recv()
                    left_send[shard, p] = (value + left_recv[shard, p].astype(F32)).astype(BF16)

                @pl.when(s == last)
                def _():
                    left_send[shard, p] = value.astype(BF16)

                copy.start()

        return carry

    lax.fori_loop(0, last, step, 0)
    for p in range(PARTS):
        cols = slice(p * PCOL, (p + 1) * PCOL)
        total[:, cols] = partial(s, p)

        @pl.when(s > 0)
        def _():
            hop(s, p, right_send, right_recv, right_s, right_r, up).wait_recv()
            total[:, cols] = total[:, cols] + right_recv[s, p].astype(F32)

        @pl.when(s < last)
        def _():
            hop(s, p, left_send, left_recv, left_s, left_r, down).wait_recv()
            total[:, cols] = total[:, cols] + left_recv[s, p].astype(F32)

    for copy in a_near + [a_far] + a_pass + u_near + [u_far] + u_pass:
        copy.wait_send()

    @pl.when(s > 0)
    def _():
        u_shift.wait_send()

    for copy in ca_near + ca_far + cu_near + cu_far + peak_x + [peak_z] + g_y + [g_core] + g_pass:
        copy.wait_send()
    for k in range(3):
        send(send_a.at[0], recv_a.at[k], ring_s.at[k], ring_r.at[k], at_y(k + 1)).wait_send()
        send(send_u.at[0], recv_u.at[k], ring_s.at[3 + k], ring_r.at[3 + k], at_y(k + 1)).wait_send()

    def drain(shard, carry):
        for p in range(PARTS):

            @pl.when(shard > s)
            def _():
                hop(shard, p, right_send, right_recv, right_s, right_r, up).wait_send()

            @pl.when(shard < s)
            def _():
                hop(shard, p, left_send, left_recv, left_s, left_r, down).wait_send()

        return carry

    lax.fori_loop(0, n_sec, drain, 0)


def body(acts, incoming, rotation, q_weight, w_exponents):
    any_ref = pl.BlockSpec(memory_space=pl.ANY)
    vmem = pl.BlockSpec(memory_space=pltpu.VMEM)
    dma = pltpu.SemaphoreType.DMA
    n_sec = lax.axis_size("section")
    hops = (n_sec, PARTS, SHARD, PCOL)
    total, grad = pl.pallas_call(
        kernel,
        name="rotation_gradient",
        out_shape=(
            jax.ShapeDtypeStruct((SHARD, WIDE), F32),
            jax.ShapeDtypeStruct((1, TOK, WIDE), BF16),
        ),
        in_specs=[any_ref, any_ref, any_ref, any_ref, vmem],
        out_specs=(vmem, vmem),
        scratch_shapes=[
            pltpu.VMEM((8 * TOK, WIDE), BF16),
            pltpu.VMEM((8 * TOK, WIDE), BF16),
            pltpu.VMEM((WIDE, WIDE), BF16),
            pltpu.VMEM((WIDE, WIDE), BF16),
            pltpu.VMEM((WIDE, WIDE), BF16),
            pltpu.VMEM((WIDE, 8 * TOK), BF16),
            pltpu.VMEM((8 * TOK, WIDE), BF16),
            pltpu.VMEM((8 * TOK, WIDE), BF16),
            pltpu.VMEM((NY, TOK, WIDE), BF16),
            pltpu.VMEM((NY, TOK, WIDE), BF16),
            pltpu.VMEM((NY, TOK, WIDE), BF16),
            pltpu.VMEM((NY, TOK, WIDE), BF16),
            pltpu.VMEM((3, TOK, WIDE), BF16),
            pltpu.VMEM((3, TOK, WIDE), BF16),
            pltpu.VMEM((TOK, WIDE), F32),
            pltpu.VMEM((TOK, WIDE), F32),
            pltpu.VMEM((2, 8, 128), F32),
            pltpu.VMEM((4, 8, 128), F32),
            pltpu.VMEM((TOK, WIDE), F32),
            pltpu.VMEM((8 * TOK, WIDE), BF16),
            pltpu.VMEM(hops, BF16),
            pltpu.VMEM(hops, BF16),
            pltpu.VMEM(hops, BF16),
            pltpu.VMEM(hops, BF16),
            dma((4,)),
            dma((7,)), dma((7,)), dma((8,)), dma((8,)),
            dma((8,)), dma((8,)), dma((6,)), dma((6,)),
            dma((4,)), dma((4,)), dma((7,)), dma((7,)),
            dma((n_sec, PARTS)), dma((n_sec, PARTS)),
            dma((n_sec, PARTS)), dma((n_sec, PARTS)),
        ],
        compiler_params=pltpu.CompilerParams(
            collective_id=0, has_side_effects=True, vmem_limit_bytes=48 * 2**20
        ),
        cost_estimate=pl.CostEstimate(
            flops=3 * 2 * 512 * WIDE * WIDE, bytes_accessed=6 * 2**20, transcendentals=2**20
        ),
    )(acts, incoming, rotation, q_weight, w_exponents)
    return total, grad


def solution(mesh):
    placed = (
        P("section", "seq", "tensor"),
        P("section", "seq", "tensor"),
        P("tensor", "seq"),
        P("section", "seq", "tensor"),
        P("section", "tensor"),
    )
    return jax.shard_map(
        body,
        mesh=mesh,
        in_specs=placed,
        out_specs=(P(("tensor", "section"), "seq"), P("section", "tensor", "seq")),
        check_vma=False,
    )
```

```python
import jax
import jax.numpy as jnp
from jax import lax
from jax.experimental import pallas as pl
from jax.experimental.pallas import tpu as pltpu
from jax.sharding import PartitionSpec as P

F32, BF16 = jnp.float32, jnp.bfloat16
ACT_CLIP = 0.5
NX, NY = 4, 4
TOK = 64
WIDE = 1024
SHARD = 128
PARTS = 2
PCOL = WIDE // PARTS
TILE = 256
HALF = TOK // 2


def kernel(
    acts, incoming, rotation, weight, expos,
    total, grad_out,
    tok_a, tok_u, rot_v, w_v, quant, acts_t,
    prod_a, prod_u, core_a, core_u, send_a, send_u, recv_a, recv_u,
    own_a, own_u, peak_own, peak_recv, gate, grads,
    right_send, right_recv, left_send, left_recv,
    local_sem, gather_a_s, gather_a_r, gather_u_s, gather_u_r,
    core_s, core_r, ring_s, ring_r, peak_s, peak_r, grad_s, grad_r,
    right_s, right_r, left_s, left_r,
):
    n_sec = lax.axis_size("section")
    s = lax.axis_index("section")
    q = lax.axis_index("seq")
    t = lax.axis_index("tensor")
    zh, x = q // NX, q % NX
    y, c = t // 2, t % 2
    last = n_sec - 1

    def at_x(k):
        return (s, zh * NX + (x + k) % NX, t)

    def at_y(k):
        return (s, q, ((y + k) % NY) * 2 + c)

    def at_far(k):
        return (s, (1 - zh) * NX + (x + k) % NX, t)

    far = at_far(0)
    mate = (s, q, y * 2 + 1 - c)
    up, down = (s + 1, q, t), (s - 1, q, t)

    def signal(device):
        pl.semaphore_signal(barrier, inc=1, device_id=device, device_id_type=pl.DeviceIdType.MESH)

    def send(src, dst, ssem, rsem, device):
        return pltpu.make_async_remote_copy(
            src_ref=src, dst_ref=dst, send_sem=ssem, recv_sem=rsem,
            device_id=device, device_id_type=pl.DeviceIdType.MESH,
        )

    def rows(block, size=TOK):
        return pl.ds(pl.multiple_of(block * size, size), size)

    load_rot = pltpu.make_async_copy(rotation, rot_v, local_sem.at[0])
    load_w = pltpu.make_async_copy(weight.at[0], w_v, local_sem.at[1])
    load_a = pltpu.make_async_copy(acts.at[0], tok_a.at[rows(q)], local_sem.at[2])
    load_u = pltpu.make_async_copy(incoming.at[0], tok_u.at[rows(q)], local_sem.at[3])
    load_a.start()
    load_w.start()
    load_rot.start()

    @pl.when(s == last)
    def _():
        load_u.start()

    barrier = pltpu.get_barrier_semaphore()
    for k in (1, 2, 3):
        signal(at_x(k))
        signal(at_y(k))
    for k in range(4):
        signal(at_far(k))
    signal(mate)

    @pl.when(s < last)
    def _():
        signal(up)

    @pl.when(s > 0)
    def _():
        signal(down)

    load_w.wait()
    scale = 127.0 * jnp.exp2(expos[...].astype(F32))
    inverse = 1.0 / scale

    def quantize(i, carry):
        r = rows(i, 64)
        quant[r] = (scale * jnp.tanh(w_v[r].astype(F32) * inverse)).astype(BF16)
        return carry

    lax.fori_loop(0, WIDE // 64, quantize, 0)
    pl.semaphore_wait(
        barrier, 11 + jnp.where(s < last, 1, 0) + jnp.where(s > 0, 1, 0)
    )

    mine = rows(q)

    def piece(block, h):
        return pl.ds(pl.multiple_of(block * TOK + h * HALF, HALF), HALF)

    def gather(first, tok, ssem, rsem):
        other = (1 - zh) * NX + x
        near = [
            send(first, tok.at[mine], ssem.at[k - 1], rsem.at[k - 1], at_x(k)) for k in (1, 2, 3)
        ]
        across = [
            send(
                first.at[pl.ds(h * HALF, HALF)], tok.at[piece(q, h)],
                ssem.at[3 + h], rsem.at[3 + h], far,
            )
            for h in (0, 1)
        ]
        onward = [
            [
                send(
                    tok.at[piece(other, h)], tok.at[piece(other, h)],
                    ssem.at[4 + 3 * h + k], rsem.at[4 + 3 * h + k], at_x(k),
                )
                for k in (1, 2, 3)
            ]
            for h in (0, 1)
        ]
        return near, across, onward

    a_near, a_far, a_pass = gather(acts.at[0], tok_a, gather_a_s, gather_a_r)
    u_near, u_far, u_pass = gather(tok_u.at[mine], tok_u, gather_u_s, gather_u_r)
    u_shift = send(incoming.at[0], tok_u.at[mine], gather_u_s.at[11], gather_u_r.at[11], down)

    def relay(arriving, onward):
        arriving.wait_recv()
        for copy in onward:
            copy.start()

    @pl.when(s > 0)
    def _():
        u_shift.start()

    a_far[0].start()
    for copy in a_near:
        copy.start()

    @pl.when(s < last)
    def _():
        u_shift.wait_recv()

    @pl.when(s == last)
    def _():
        load_u.wait()

    for copy in u_near:
        copy.start()

    load_rot.wait()
    load_a.wait()

    def follow(done, copy):
        done.wait_send()
        copy.start()

    every = (0, WIDE)
    parts = [(p * PCOL, PCOL) for p in range(PARTS)]

    def project(half, tok, mat, flip, prod, core_in, base, cols):
        r = pl.ds(pl.multiple_of(half * (NX * TOK), NX * TOK), NX * TOK)

        def tile(n, carry):
            at = pl.ds(pl.multiple_of(cols[0] + n * TILE, TILE), TILE)
            if flip:
                value = lax.dot_general(
                    tok[r], mat[at], (((1,), (1,)), ((), ())), preferred_element_type=F32
                )
            else:
                value = jnp.dot(tok[r], mat[:, at], preferred_element_type=F32)
            prod[r, at] = value.astype(BF16)
            return carry

        lax.fori_loop(0, cols[1] // TILE, tile, 0)
        copies = []
        for j in (0, 1):
            chip = half * 2 + j
            copy = send(
                prod.at[rows(chip * 2 + 1 - c), pl.ds(*cols)], core_in.at[chip, :, pl.ds(*cols)],
                core_s.at[base + j], core_r.at[base + j], mate,
            )
            copy.start()
            copies.append(copy)
        return copies

    def scatter(half, copies, prod, core_in, out, landing, own, base, cols):
        at = pl.ds(*cols)
        for j in (0, 1):
            chip = half * 2 + j
            copies[j].wait_recv()
            both = prod[rows(chip * 2 + c), at].astype(F32) + core_in[chip, :, at].astype(F32)

            @pl.when(chip == y)
            def _():
                own[:, at] = both

            @pl.when(chip != y)
            def _():
                k = (chip - y + NY) % NY - 1
                out[chip, :, at] = both.astype(BF16)
                send(
                    out.at[chip, :, at], landing.at[k, :, at],
                    ring_s.at[base + k], ring_r.at[base + k], (s, q, chip * 2 + c),
                ).start()

    def ring(k, out, landing, base, cols):
        at = pl.ds(*cols)
        return send(
            out.at[0, :, at], landing.at[k, :, at],
            ring_s.at[base + k], ring_r.at[base + k], at_y(k + 1),
        )

    def collect(out, landing, own, base, cols):
        at = pl.ds(*cols)
        value = own[:, at]
        for k in range(3):
            ring(k, out, landing, base, cols).wait_recv()
            value = value + landing[k, :, at].astype(F32)
        return value

    near_half, far_half = zh, 1 - zh
    def project_u(half, base):
        return [
            project(half, tok_u, quant, True, prod_u, core_u, base + 2 * p, parts[p])
            for p in range(PARTS)
        ]

    def scatter_u(half, copies):
        for p in range(PARTS):
            scatter(
                half, copies[p], prod_u, core_u, send_u, recv_u, own_u, 3 + 3 * p, parts[p]
            )

    follow(a_far[0], a_far[1])
    for copy in a_near:
        copy.wait_recv()
    ca_near = project(near_half, tok_a, rot_v, False, prod_a, core_a, 0, every)
    follow(a_far[1], u_far[0])
    relay(a_far[0], a_pass[0])
    for copy in u_near:
        copy.wait_recv()
    cu_near = project_u(near_half, 4)
    scatter(near_half, ca_near, prod_a, core_a, send_a, recv_a, own_a, 0, every)
    relay(a_far[1], a_pass[1])
    follow(u_far[0], u_far[1])
    scatter_u(near_half, cu_near)
    for copy in a_pass[0] + a_pass[1]:
        copy.wait_recv()
    ca_far = project(far_half, tok_a, rot_v, False, prod_a, core_a, 2, every)
    scatter(far_half, ca_far, prod_a, core_a, send_a, recv_a, own_a, 0, every)
    relay(u_far[0], u_pass[0])

    rotated = collect(send_a, recv_a, own_a, 0, every)
    own_a[...] = rotated
    diagonal = lax.broadcasted_iota(jnp.int32, (TOK, 128), 0) == lax.broadcasted_iota(
        jnp.int32, (TOK, 128), 1
    )
    peak = jnp.max(jnp.abs(rotated), axis=1, keepdims=True)
    line = jnp.max(jnp.where(diagonal, peak, 0.0), axis=0, keepdims=True)
    peak_own[...] = jnp.broadcast_to(line, (8, 128))
    peaks = [
        send(peak_own, peak_recv.at[i], peak_s.at[i], peak_r.at[i], device)
        for i, device in enumerate([at_x(k) for k in (1, 2, 3)] + [at_far(k) for k in range(4)])
    ]
    for copy in reversed(peaks):
        copy.start()
    relay(u_far[1], u_pass[1])

    def turn(i, carry):
        r = pl.ds(pl.multiple_of(i * 128, 128), 128)
        acts_t[r] = tok_a[:, r].T
        return carry

    lax.fori_loop(0, WIDE // 128, turn, 0)
    for copy in u_pass[0] + u_pass[1]:
        copy.wait_recv()
    cu_far = project_u(far_half, 8)
    scatter_u(far_half, cu_far)
    for copy in peaks:
        copy.wait_recv()
    line = jnp.maximum(peak_own[...], jnp.max(peak_recv[...], axis=0))[0:1]
    peak = jnp.max(jnp.where(diagonal, line, 0.0), axis=1, keepdims=True)
    clip = ACT_CLIP * (peak + 1e-06)
    ratio = jnp.tanh(own_a[...] * (1.0 / clip))
    gate[...] = 1.0 - ratio * ratio

    def part(block, p):
        return grads.at[rows(block), pl.ds(*parts[p])]

    g_y, g_core, g_pass = [], [], []
    for p in range(PARTS):
        at = pl.ds(*parts[p])
        back = collect(send_u, recv_u, own_u, 3 + 3 * p, parts[p])
        grad = (back * gate[:, at]).astype(BF16)
        grads[rows(t), at] = grad
        grad_out[0, :, at] = grad
        base = 7 * p
        g_y.append([
            send(part(t, p), part(t, p), grad_s.at[base + k], grad_r.at[base + k], at_y(k))
            for k in (1, 2, 3)
        ])
        g_core.append(send(part(t, p), part(t, p), grad_s.at[base], grad_r.at[base], mate))
        for copy in g_y[p] + [g_core[p]]:
            copy.start()
        passing = []
        for k in (1, 2, 3):
            block = ((y - k + NY) % NY) * 2 + c
            i = base + 3 + k
            passing.append(send(part(block, p), part(block, p), grad_s.at[i], grad_r.at[i], mate))
        g_pass.append(passing)

    def assemble(p):
        for arrived, onward in zip(g_y[p], g_pass[p]):
            arrived.wait_recv()
            onward.start()
        for copy in [g_core[p]] + g_pass[p]:
            copy.wait_recv()

    def partial(shard, p):
        return jnp.dot(
            acts_t[rows(shard, SHARD)], grads[:, p * PCOL : (p + 1) * PCOL],
            preferred_element_type=F32,
        )

    def hop(shard, p, out, landing, ssem, rsem, device):
        return send(
            out.at[shard, p], landing.at[shard, p], ssem.at[shard, p], rsem.at[shard, p], device
        )

    def step(tau, p):
        @pl.when(tau >= s)
        def _():
            shard = last - (tau - s)
            value = partial(shard, p)
            copy = hop(shard, p, right_send, right_recv, right_s, right_r, up)

            @pl.when(s > 0)
            def _():
                copy.wait_recv()
                right_send[shard, p] = (value + right_recv[shard, p].astype(F32)).astype(BF16)

            @pl.when(s == 0)
            def _():
                right_send[shard, p] = value.astype(BF16)

            copy.start()

        @pl.when(tau >= last - s)
        def _():
            shard = tau - (last - s)
            value = partial(shard, p)
            copy = hop(shard, p, left_send, left_recv, left_s, left_r, down)

            @pl.when(s < last)
            def _():
                copy.wait_recv()
                left_send[shard, p] = (value + left_recv[shard, p].astype(F32)).astype(BF16)

            @pl.when(s == last)
            def _():
                left_send[shard, p] = value.astype(BF16)

            copy.start()

    assemble(0)
    step(0, 0)
    assemble(1)
    step(0, 1)

    def steps(tau, carry):
        for p in range(PARTS):
            step(tau, p)
        return carry

    lax.fori_loop(1, last, steps, 0)
    for p in range(PARTS):
        cols = slice(p * PCOL, (p + 1) * PCOL)
        total[:, cols] = partial(s, p)

        @pl.when(s > 0)
        def _():
            hop(s, p, right_send, right_recv, right_s, right_r, up).wait_recv()
            total[:, cols] = total[:, cols] + right_recv[s, p].astype(F32)

        @pl.when(s < last)
        def _():
            hop(s, p, left_send, left_recv, left_s, left_r, down).wait_recv()
            total[:, cols] = total[:, cols] + left_recv[s, p].astype(F32)

    for copy in a_pass[0] + a_pass[1] + u_near + u_far[1:] + u_pass[0] + u_pass[1]:
        copy.wait_send()

    @pl.when(s > 0)
    def _():
        u_shift.wait_send()

    for copy in a_near + ca_far + sum(cu_near + cu_far, ca_near) + peaks:
        copy.wait_send()
    for p in range(PARTS):
        for copy in g_y[p] + [g_core[p]] + g_pass[p]:
            copy.wait_send()
    for k in range(3):
        ring(k, send_a, recv_a, 0, every).wait_send()
        for p in range(PARTS):
            ring(k, send_u, recv_u, 3 + 3 * p, parts[p]).wait_send()

    def drain(shard, carry):
        for p in range(PARTS):

            @pl.when(shard > s)
            def _():
                hop(shard, p, right_send, right_recv, right_s, right_r, up).wait_send()

            @pl.when(shard < s)
            def _():
                hop(shard, p, left_send, left_recv, left_s, left_r, down).wait_send()

        return carry

    lax.fori_loop(0, n_sec, drain, 0)


def body(acts, incoming, rotation, q_weight, w_exponents):
    hbm = pl.BlockSpec(memory_space=pltpu.HBM)
    vmem = pl.BlockSpec(memory_space=pltpu.VMEM)
    dma = pltpu.SemaphoreType.DMA
    n_sec = lax.axis_size("section")
    hops = (n_sec, PARTS, SHARD, PCOL)
    total, grad = pl.pallas_call(
        kernel,
        name="rotation_gradient",
        out_shape=(
            jax.ShapeDtypeStruct((SHARD, WIDE), F32),
            jax.ShapeDtypeStruct((1, TOK, WIDE), BF16),
        ),
        in_specs=[hbm, hbm, hbm, hbm, vmem],
        out_specs=(vmem, vmem),
        scratch_shapes=[
            pltpu.VMEM((8 * TOK, WIDE), BF16),
            pltpu.VMEM((8 * TOK, WIDE), BF16),
            pltpu.VMEM((WIDE, WIDE), BF16),
            pltpu.VMEM((WIDE, WIDE), BF16),
            pltpu.VMEM((WIDE, WIDE), BF16),
            pltpu.VMEM((WIDE, 8 * TOK), BF16),
            pltpu.VMEM((8 * TOK, WIDE), BF16),
            pltpu.VMEM((8 * TOK, WIDE), BF16),
            pltpu.VMEM((NY, TOK, WIDE), BF16),
            pltpu.VMEM((NY, TOK, WIDE), BF16),
            pltpu.VMEM((NY, TOK, WIDE), BF16),
            pltpu.VMEM((NY, TOK, WIDE), BF16),
            pltpu.VMEM((3, TOK, WIDE), BF16),
            pltpu.VMEM((3, TOK, WIDE), BF16),
            pltpu.VMEM((TOK, WIDE), F32),
            pltpu.VMEM((TOK, WIDE), F32),
            pltpu.VMEM((8, 128), F32),
            pltpu.VMEM((7, 8, 128), F32),
            pltpu.VMEM((TOK, WIDE), F32),
            pltpu.VMEM((8 * TOK, WIDE), BF16),
            pltpu.VMEM(hops, BF16),
            pltpu.VMEM(hops, BF16),
            pltpu.VMEM(hops, BF16),
            pltpu.VMEM(hops, BF16),
            dma((4,)),
            dma((11,)), dma((11,)), dma((12,)), dma((12,)),
            dma((12,)), dma((12,)), dma((3 + 3 * PARTS,)), dma((3 + 3 * PARTS,)),
            dma((7,)), dma((7,)), dma((7 * PARTS,)), dma((7 * PARTS,)),
            dma((n_sec, PARTS)), dma((n_sec, PARTS)),
            dma((n_sec, PARTS)), dma((n_sec, PARTS)),
        ],
        compiler_params=pltpu.CompilerParams(
            collective_id=0, has_side_effects=True, vmem_limit_bytes=63 * 2**20
        ),
        cost_estimate=pl.CostEstimate(
            flops=3 * 2 * 512 * WIDE * WIDE, bytes_accessed=6 * 2**20, transcendentals=2**20
        ),
    )(acts, incoming, rotation, q_weight, w_exponents)
    return total, grad


def solution(mesh):
    placed = (
        P("section", "seq", "tensor"),
        P("section", "seq", "tensor"),
        P("tensor", "seq"),
        P("section", "seq", "tensor"),
        P("section", "tensor"),
    )
    return jax.shard_map(
        body,
        mesh=mesh,
        in_specs=placed,
        out_specs=(P(("tensor", "section"), "seq"), P("section", "tensor", "seq")),
        check_vma=False,
    )
```

```python
import jax
import jax.numpy as jnp
from jax import lax
from jax.experimental import pallas as pl
from jax.experimental.pallas import tpu as pltpu
from jax.sharding import PartitionSpec as P

F32, BF16 = jnp.float32, jnp.bfloat16
ACT_CLIP = 0.5
VMEM_LIMIT = 63 * 2**20
NX, NY = 4, 4
TOK = 64
WIDE = 1024
SHARD = 128
PARTS = 4
PCOL = WIDE // PARTS
TILE = 256
HALF = TOK // 2


def kernel(
    acts, incoming, rotation, weight, expos,
    total, grad_out,
    tok_a, tok_u, rot_v, w_v, quant, acts_t,
    prod_a, prod_u, core_a, core_u, send_a, send_u, recv_a, recv_u,
    own_a, own_u, peak_own, peak_recv, gate, grads,
    right_send, right_recv, left_send, left_recv,
    local_sem, gather_a_s, gather_a_r, gather_u_s, gather_u_r,
    core_s, core_r, ring_s, ring_r, peak_s, peak_r, grad_s, grad_r,
    right_s, right_r, left_s, left_r,
):
    n_sec = lax.axis_size("section")
    s = lax.axis_index("section")
    q = lax.axis_index("seq")
    t = lax.axis_index("tensor")
    zh, x = q // NX, q % NX
    y, c = t // 2, t % 2
    last = n_sec - 1

    def at_x(k):
        return (s, zh * NX + (x + k) % NX, t)

    def at_y(k):
        return (s, q, ((y + k) % NY) * 2 + c)

    def at_far(k):
        return (s, (1 - zh) * NX + (x + k) % NX, t)

    far = at_far(0)
    mate = (s, q, y * 2 + 1 - c)
    up, down = (s + 1, q, t), (s - 1, q, t)

    def signal(device):
        pl.semaphore_signal(barrier, inc=1, device_id=device, device_id_type=pl.DeviceIdType.MESH)

    def send(src, dst, ssem, rsem, device):
        return pltpu.make_async_remote_copy(
            src_ref=src, dst_ref=dst, send_sem=ssem, recv_sem=rsem,
            device_id=device, device_id_type=pl.DeviceIdType.MESH,
        )

    def rows(block, size=TOK):
        return pl.ds(pl.multiple_of(block * size, size), size)

    load_rot = pltpu.make_async_copy(rotation, rot_v, local_sem.at[0])
    load_w = pltpu.make_async_copy(weight.at[0], w_v, local_sem.at[1])
    load_a = pltpu.make_async_copy(acts.at[0], tok_a.at[rows(q)], local_sem.at[2])
    load_u = pltpu.make_async_copy(incoming.at[0], tok_u.at[rows(q)], local_sem.at[3])
    load_a.start()
    load_w.start()
    load_rot.start()

    @pl.when(s == last)
    def _():
        load_u.start()

    barrier = pltpu.get_barrier_semaphore()
    for k in (1, 2, 3):
        signal(at_x(k))
        signal(at_y(k))
    for k in range(4):
        signal(at_far(k))
    signal(mate)

    @pl.when(s < last)
    def _():
        signal(up)

    @pl.when(s > 0)
    def _():
        signal(down)

    load_w.wait()
    scale = 127.0 * jnp.exp2(expos[...].astype(F32))
    inverse = 1.0 / scale

    def quantize(i, carry):
        r = rows(i, 64)
        quant[r] = (scale * jnp.tanh(w_v[r].astype(F32) * inverse)).astype(BF16)
        return carry

    lax.fori_loop(0, WIDE // 64, quantize, 0)
    pl.semaphore_wait(
        barrier, 11 + jnp.where(s < last, 1, 0) + jnp.where(s > 0, 1, 0)
    )

    mine = rows(q)

    def piece(block, h):
        return pl.ds(pl.multiple_of(block * TOK + h * HALF, HALF), HALF)

    def gather(first, tok, ssem, rsem):
        other = (1 - zh) * NX + x
        near = [
            send(first, tok.at[mine], ssem.at[k - 1], rsem.at[k - 1], at_x(k)) for k in (1, 2, 3)
        ]
        across = [
            send(
                first.at[pl.ds(h * HALF, HALF)], tok.at[piece(q, h)],
                ssem.at[3 + h], rsem.at[3 + h], far,
            )
            for h in (0, 1)
        ]
        onward = [
            [
                send(
                    tok.at[piece(other, h)], tok.at[piece(other, h)],
                    ssem.at[4 + 3 * h + k], rsem.at[4 + 3 * h + k], at_x(k),
                )
                for k in (1, 2, 3)
            ]
            for h in (0, 1)
        ]
        return near, across, onward

    a_near, a_far, a_pass = gather(acts.at[0], tok_a, gather_a_s, gather_a_r)
    u_near, u_far, u_pass = gather(tok_u.at[mine], tok_u, gather_u_s, gather_u_r)
    u_shift = send(incoming.at[0], tok_u.at[mine], gather_u_s.at[11], gather_u_r.at[11], down)

    def relay(arriving, onward):
        arriving.wait_recv()
        for copy in onward:
            copy.start()

    @pl.when(s > 0)
    def _():
        u_shift.start()

    a_far[0].start()
    for copy in a_near:
        copy.start()

    @pl.when(s < last)
    def _():
        u_shift.wait_recv()

    @pl.when(s == last)
    def _():
        load_u.wait()

    for copy in u_near:
        copy.start()

    load_rot.wait()
    load_a.wait()

    def follow(done, copy):
        done.wait_send()
        copy.start()

    parts = [(p * PCOL, PCOL) for p in range(PARTS)]

    def project(half, h, tok, mat, flip, prod, core_in, base):
        value = jnp.concatenate([tok[piece(half * NX + i, h)] for i in range(NX)], axis=0)

        def tile(n, carry):
            at = pl.ds(pl.multiple_of(n * TILE, TILE), TILE)
            if flip:
                result = lax.dot_general(
                    value, mat[at], (((1,), (1,)), ((), ())), preferred_element_type=F32
                )
            else:
                result = jnp.dot(value, mat[:, at], preferred_element_type=F32)
            for i in range(NX):
                prod[piece(half * NX + i, h), at] = result[i * HALF : (i + 1) * HALF].astype(BF16)
            return carry

        lax.fori_loop(0, WIDE // TILE, tile, 0)
        copies = []
        for j in (0, 1):
            chip = half * 2 + j
            copy = send(
                prod.at[piece(chip * 2 + 1 - c, h)], core_in.at[chip, pl.ds(h * HALF, HALF)],
                core_s.at[base + j], core_r.at[base + j], mate,
            )
            copy.start()
            copies.append(copy)
        return copies

    def scatter(half, h, copies, prod, core_in, out, landing, own, base):
        at = pl.ds(h * HALF, HALF)
        for j in (0, 1):
            chip = half * 2 + j
            copies[j].wait_recv()
            both = prod[piece(chip * 2 + c, h)].astype(F32) + core_in[chip, at].astype(F32)

            @pl.when(chip == y)
            def _():
                own[at] = both

            @pl.when(chip != y)
            def _():
                k = (chip - y + NY) % NY - 1
                out[chip, at] = both.astype(BF16)
                send(
                    out.at[chip, at], landing.at[k, at],
                    ring_s.at[base + k], ring_r.at[base + k], (s, q, chip * 2 + c),
                ).start()

    def ring(k, h, out, landing, base):
        at = pl.ds(h * HALF, HALF)
        return send(
            out.at[0, at], landing.at[k, at],
            ring_s.at[base + k], ring_r.at[base + k], at_y(k + 1),
        )

    def collect(out, landing, own, base):
        value = own[...]
        for k in range(3):
            for h in (0, 1):
                ring(k, h, out, landing, base + 3 * h).wait_recv()
            value = value + landing[k].astype(F32)
        return value

    near_half, far_half = zh, 1 - zh

    def project_a(half, h, base):
        return project(half, h, tok_a, rot_v, False, prod_a, core_a, base)

    def project_u(half, h, base):
        return project(half, h, tok_u, quant, True, prod_u, core_u, base)

    def scatter_a(half, h, copies):
        scatter(half, h, copies, prod_a, core_a, send_a, recv_a, own_a, 3 * h)

    def scatter_u(half, h, copies):
        scatter(half, h, copies, prod_u, core_u, send_u, recv_u, own_u, 6 + 3 * h)

    def arrive(copies):
        for copy in copies:
            copy.wait_recv()

    follow(a_far[0], a_far[1])
    arrive(a_near)
    mates = [project_a(near_half, 0, 0), project_a(near_half, 1, 2)]
    follow(a_far[1], u_far[0])
    relay(a_far[0], a_pass[0])
    scatter_a(near_half, 0, mates[0])
    scatter_a(near_half, 1, mates[1])
    arrive(u_near)
    mates += [project_u(near_half, 0, 8), project_u(near_half, 1, 10)]
    arrive(a_pass[0])
    mates.append(project_a(far_half, 0, 4))
    relay(a_far[1], a_pass[1])
    follow(u_far[0], u_far[1])
    scatter_a(far_half, 0, mates[4])
    scatter_u(near_half, 0, mates[2])
    scatter_u(near_half, 1, mates[3])
    arrive(a_pass[1])
    mates.append(project_a(far_half, 1, 6))
    relay(u_far[0], u_pass[0])
    scatter_a(far_half, 1, mates[5])
    relay(u_far[1], u_pass[1])

    rotated = collect(send_a, recv_a, own_a, 0)
    own_a[...] = rotated
    peak = jnp.max(jnp.abs(rotated), axis=1, keepdims=True)
    diagonal = lax.broadcasted_iota(jnp.int32, (TOK, 128), 0) == lax.broadcasted_iota(
        jnp.int32, (TOK, 128), 1
    )
    line = jnp.max(jnp.where(diagonal, peak, 0.0), axis=0, keepdims=True)
    peak_own[...] = jnp.broadcast_to(line, (8, 128))
    peaks = [
        send(peak_own, peak_recv.at[i], peak_s.at[i], peak_r.at[i], device)
        for i, device in enumerate([at_x(k) for k in (1, 2, 3)] + [at_far(k) for k in range(4)])
    ]
    for copy in reversed(peaks):
        copy.start()
    for h in (0, 1):
        arrive(u_pass[h])
        mates.append(project_u(far_half, h, 12 + 2 * h))
        scatter_u(far_half, h, mates[-1])

    def turn(i, carry):
        r = pl.ds(pl.multiple_of(i * 128, 128), 128)
        acts_t[r] = tok_a[:, r].T
        return carry

    lax.fori_loop(0, WIDE // 128, turn, 0)
    for copy in peaks:
        copy.wait_recv()
    line = jnp.maximum(peak_own[...], jnp.max(peak_recv[...], axis=0))[0:1]
    peak = jnp.max(jnp.where(diagonal, line, 0.0), axis=1, keepdims=True)
    clip = ACT_CLIP * (peak + 1e-06)
    ratio = jnp.tanh(own_a[...] * (1.0 / clip))
    gate[...] = 1.0 - ratio * ratio

    def part(block, p):
        return grads.at[rows(block), pl.ds(*parts[p])]

    back = collect(send_u, recv_u, own_u, 6)
    g_y, g_core, g_pass = [], [], []
    for p in range(PARTS):
        at = pl.ds(*parts[p])
        grad = (back[:, p * PCOL : (p + 1) * PCOL] * gate[:, at]).astype(BF16)
        grads[rows(t), at] = grad
        grad_out[0, :, at] = grad
        base = 7 * p
        g_y.append([
            send(part(t, p), part(t, p), grad_s.at[base + k], grad_r.at[base + k], at_y(k))
            for k in (1, 2, 3)
        ])
        g_core.append(send(part(t, p), part(t, p), grad_s.at[base], grad_r.at[base], mate))
        for copy in g_y[p] + [g_core[p]]:
            copy.start()
        passing = []
        for k in (1, 2, 3):
            block = ((y - k + NY) % NY) * 2 + c
            i = base + 3 + k
            passing.append(send(part(block, p), part(block, p), grad_s.at[i], grad_r.at[i], mate))
        g_pass.append(passing)

    def assemble(p):
        for arrived, onward in zip(g_y[p], g_pass[p]):
            arrived.wait_recv()
            onward.start()
        for copy in [g_core[p]] + g_pass[p]:
            copy.wait_recv()

    def partial(shard, p):
        return jnp.dot(
            acts_t[rows(shard, SHARD)], grads[:, p * PCOL : (p + 1) * PCOL],
            preferred_element_type=F32,
        )

    def hop(shard, p, out, landing, ssem, rsem, device):
        return send(
            out.at[shard, p], landing.at[shard, p], ssem.at[shard, p], rsem.at[shard, p], device
        )

    def step(tau, p):
        @pl.when(tau >= s)
        def _():
            shard = last - (tau - s)
            value = partial(shard, p)
            copy = hop(shard, p, right_send, right_recv, right_s, right_r, up)

            @pl.when(s > 0)
            def _():
                copy.wait_recv()
                right_send[shard, p] = (value + right_recv[shard, p].astype(F32)).astype(BF16)

            @pl.when(s == 0)
            def _():
                right_send[shard, p] = value.astype(BF16)

            copy.start()

        @pl.when(tau >= last - s)
        def _():
            shard = tau - (last - s)
            value = partial(shard, p)
            copy = hop(shard, p, left_send, left_recv, left_s, left_r, down)

            @pl.when(s < last)
            def _():
                copy.wait_recv()
                left_send[shard, p] = (value + left_recv[shard, p].astype(F32)).astype(BF16)

            @pl.when(s == last)
            def _():
                left_send[shard, p] = value.astype(BF16)

            copy.start()

    for p in range(PARTS):
        assemble(p)
        step(0, p)

    def steps(tau, carry):
        for p in range(PARTS):
            step(tau, p)
        return carry

    lax.fori_loop(1, last, steps, 0)
    for p in range(PARTS):
        cols = slice(p * PCOL, (p + 1) * PCOL)
        total[:, cols] = partial(s, p)

        @pl.when(s > 0)
        def _():
            hop(s, p, right_send, right_recv, right_s, right_r, up).wait_recv()
            total[:, cols] = total[:, cols] + right_recv[s, p].astype(F32)

        @pl.when(s < last)
        def _():
            hop(s, p, left_send, left_recv, left_s, left_r, down).wait_recv()
            total[:, cols] = total[:, cols] + left_recv[s, p].astype(F32)

    for copy in a_pass[0] + a_pass[1] + u_near + u_far[1:] + u_pass[0] + u_pass[1]:
        copy.wait_send()

    @pl.when(s > 0)
    def _():
        u_shift.wait_send()

    for copy in a_near + sum(mates, peaks):
        copy.wait_send()
    for p in range(PARTS):
        for copy in g_y[p] + [g_core[p]] + g_pass[p]:
            copy.wait_send()
    for k in range(3):
        for h in (0, 1):
            ring(k, h, send_a, recv_a, 3 * h).wait_send()
            ring(k, h, send_u, recv_u, 6 + 3 * h).wait_send()

    def drain(shard, carry):
        for p in range(PARTS):

            @pl.when(shard > s)
            def _():
                hop(shard, p, right_send, right_recv, right_s, right_r, up).wait_send()

            @pl.when(shard < s)
            def _():
                hop(shard, p, left_send, left_recv, left_s, left_r, down).wait_send()

        return carry

    lax.fori_loop(0, n_sec, drain, 0)


def body(acts, incoming, rotation, q_weight, w_exponents):
    hbm = pl.BlockSpec(memory_space=pltpu.HBM)
    vmem = pl.BlockSpec(memory_space=pltpu.VMEM)
    dma = pltpu.SemaphoreType.DMA
    n_sec = lax.axis_size("section")
    hops = (n_sec, PARTS, SHARD, PCOL)
    total, grad = pl.pallas_call(
        kernel,
        name="rotation_gradient",
        out_shape=(
            jax.ShapeDtypeStruct((SHARD, WIDE), F32),
            jax.ShapeDtypeStruct((1, TOK, WIDE), BF16),
        ),
        in_specs=[hbm, hbm, hbm, hbm, vmem],
        out_specs=(vmem, vmem),
        scratch_shapes=[
            pltpu.VMEM((8 * TOK, WIDE), BF16),
            pltpu.VMEM((8 * TOK, WIDE), BF16),
            pltpu.VMEM((WIDE, WIDE), BF16),
            pltpu.VMEM((WIDE, WIDE), BF16),
            pltpu.VMEM((WIDE, WIDE), BF16),
            pltpu.VMEM((WIDE, 8 * TOK), BF16),
            pltpu.VMEM((8 * TOK, WIDE), BF16),
            pltpu.VMEM((8 * TOK, WIDE), BF16),
            pltpu.VMEM((NY, TOK, WIDE), BF16),
            pltpu.VMEM((NY, TOK, WIDE), BF16),
            pltpu.VMEM((NY, TOK, WIDE), BF16),
            pltpu.VMEM((NY, TOK, WIDE), BF16),
            pltpu.VMEM((3, TOK, WIDE), BF16),
            pltpu.VMEM((3, TOK, WIDE), BF16),
            pltpu.VMEM((TOK, WIDE), F32),
            pltpu.VMEM((TOK, WIDE), F32),
            pltpu.VMEM((8, 128), F32),
            pltpu.VMEM((7, 8, 128), F32),
            pltpu.VMEM((TOK, WIDE), F32),
            pltpu.VMEM((8 * TOK, WIDE), BF16),
            pltpu.VMEM(hops, BF16),
            pltpu.VMEM(hops, BF16),
            pltpu.VMEM(hops, BF16),
            pltpu.VMEM(hops, BF16),
            dma((4,)),
            dma((11,)), dma((11,)), dma((12,)), dma((12,)),
            dma((16,)), dma((16,)), dma((12,)), dma((12,)),
            dma((7,)), dma((7,)), dma((7 * PARTS,)), dma((7 * PARTS,)),
            dma((n_sec, PARTS)), dma((n_sec, PARTS)),
            dma((n_sec, PARTS)), dma((n_sec, PARTS)),
        ],
        compiler_params=pltpu.CompilerParams(
            collective_id=0, has_side_effects=True, vmem_limit_bytes=VMEM_LIMIT
        ),
        cost_estimate=pl.CostEstimate(
            flops=3 * 2 * 512 * WIDE * WIDE, bytes_accessed=6 * 2**20, transcendentals=2**20
        ),
    )(acts, incoming, rotation, q_weight, w_exponents)
    return total, grad


def solution(mesh):
    placed = (
        P("section", "seq", "tensor"),
        P("section", "seq", "tensor"),
        P("tensor", "seq"),
        P("section", "seq", "tensor"),
        P("section", "tensor"),
    )
    return jax.shard_map(
        body,
        mesh=mesh,
        in_specs=placed,
        out_specs=(P(("tensor", "section"), "seq"), P("section", "tensor", "seq")),
        check_vma=False,
    )
```

```python
import jax
import jax.numpy as jnp
from jax import lax
from jax.experimental import pallas as pl
from jax.experimental.pallas import tpu as pltpu
from jax.sharding import PartitionSpec as P

F32, BF16 = jnp.float32, jnp.bfloat16
ACT_CLIP = 0.5
VMEM_LIMIT = 63 * 2**20
NX, NY = 4, 4
TOK = 64
WIDE = 1024
SHARD = 128
PARTS = 4
PCOL = WIDE // PARTS
TILE = 256
HALF = TOK // 2


def kernel(
    acts, incoming, rotation, weight, expos,
    total_out, grad_out,
    total, tok_a, tok_u, rot_v, w_v, quant, acts_t,
    prod_a, prod_u, core_a, core_u, send_a, send_u, recv_a, recv_u,
    own_a, own_u, peak_own, peak_recv, gate, grads,
    right_send, right_recv, left_send, left_recv,
    local_sem, gather_a_s, gather_a_r, gather_u_s, gather_u_r,
    core_s, core_r, ring_s, ring_r, peak_s, peak_r, grad_s, grad_r,
    right_s, right_r, left_s, left_r,
):
    n_sec = lax.axis_size("section")
    s = lax.axis_index("section")
    q = lax.axis_index("seq")
    t = lax.axis_index("tensor")
    zh, x = q // NX, q % NX
    y, c = t // 2, t % 2
    last = n_sec - 1

    def at_x(k):
        return (s, zh * NX + (x + k) % NX, t)

    def at_y(k):
        return (s, q, ((y + k) % NY) * 2 + c)

    def at_far(k):
        return (s, (1 - zh) * NX + (x + k) % NX, t)

    far = at_far(0)
    mate = (s, q, y * 2 + 1 - c)
    up, down = (s + 1, q, t), (s - 1, q, t)

    def signal(device):
        pl.semaphore_signal(barrier, inc=1, device_id=device, device_id_type=pl.DeviceIdType.MESH)

    def send(src, dst, ssem, rsem, device):
        return pltpu.make_async_remote_copy(
            src_ref=src, dst_ref=dst, send_sem=ssem, recv_sem=rsem,
            device_id=device, device_id_type=pl.DeviceIdType.MESH,
        )

    def rows(block, size=TOK):
        return pl.ds(pl.multiple_of(block * size, size), size)

    load_rot = pltpu.make_async_copy(rotation, rot_v, local_sem.at[0])
    load_w = pltpu.make_async_copy(weight.at[0], w_v, local_sem.at[1])
    load_a = pltpu.make_async_copy(acts.at[0], tok_a.at[rows(q)], local_sem.at[2])
    load_u = pltpu.make_async_copy(incoming.at[0], tok_u.at[rows(q)], local_sem.at[3])
    load_a.start()
    load_w.start()
    load_rot.start()

    @pl.when(s == last)
    def _():
        load_u.start()

    barrier = pltpu.get_barrier_semaphore()
    for k in (1, 2, 3):
        signal(at_x(k))
        signal(at_y(k))
    for k in range(4):
        signal(at_far(k))
    signal(mate)

    @pl.when(s < last)
    def _():
        signal(up)

    @pl.when(s > 0)
    def _():
        signal(down)

    load_w.wait()
    scale = 127.0 * jnp.exp2(expos[...].astype(F32))
    inverse = 1.0 / scale

    def quantize(i, carry):
        r = rows(i, 64)
        quant[r] = (scale * jnp.tanh(w_v[r].astype(F32) * inverse)).astype(BF16)
        return carry

    lax.fori_loop(0, WIDE // 64, quantize, 0)
    pl.semaphore_wait(
        barrier, 11 + jnp.where(s < last, 1, 0) + jnp.where(s > 0, 1, 0)
    )

    mine = rows(q)

    def piece(block, h):
        return pl.ds(pl.multiple_of(block * TOK + h * HALF, HALF), HALF)

    def gather(first, tok, ssem, rsem):
        other = (1 - zh) * NX + x
        near = [
            send(first, tok.at[mine], ssem.at[k - 1], rsem.at[k - 1], at_x(k)) for k in (1, 2, 3)
        ]
        across = [
            send(
                first.at[pl.ds(h * HALF, HALF)], tok.at[piece(q, h)],
                ssem.at[3 + h], rsem.at[3 + h], far,
            )
            for h in (0, 1)
        ]
        onward = [
            [
                send(
                    tok.at[piece(other, h)], tok.at[piece(other, h)],
                    ssem.at[4 + 3 * h + k], rsem.at[4 + 3 * h + k], at_x(k),
                )
                for k in (1, 2, 3)
            ]
            for h in (0, 1)
        ]
        return near, across, onward

    a_near, a_far, a_pass = gather(acts.at[0], tok_a, gather_a_s, gather_a_r)
    u_near, u_far, u_pass = gather(tok_u.at[mine], tok_u, gather_u_s, gather_u_r)
    u_shift = send(incoming.at[0], tok_u.at[mine], gather_u_s.at[11], gather_u_r.at[11], down)

    def relay(arriving, onward):
        arriving.wait_recv()
        for copy in onward:
            copy.start()

    @pl.when(s > 0)
    def _():
        u_shift.start()

    a_far[0].start()
    for copy in a_near:
        copy.start()

    @pl.when(s < last)
    def _():
        u_shift.wait_recv()

    @pl.when(s == last)
    def _():
        load_u.wait()

    for copy in u_near:
        copy.start()

    load_rot.wait()
    load_a.wait()

    def follow(done, copy):
        done.wait_send()
        copy.start()

    parts = [(p * PCOL, PCOL) for p in range(PARTS)]

    def project(half, h, tok, mat, flip, prod, core_in, base):
        value = jnp.concatenate([tok[piece(half * NX + i, h)] for i in range(NX)], axis=0)

        def tile(n, carry):
            at = pl.ds(pl.multiple_of(n * TILE, TILE), TILE)
            if flip:
                result = lax.dot_general(
                    value, mat[at], (((1,), (1,)), ((), ())), preferred_element_type=F32
                )
            else:
                result = jnp.dot(value, mat[:, at], preferred_element_type=F32)
            for i in range(NX):
                prod[piece(half * NX + i, h), at] = result[i * HALF : (i + 1) * HALF].astype(BF16)
            return carry

        lax.fori_loop(0, WIDE // TILE, tile, 0)
        copies = []
        for j in (0, 1):
            chip = half * 2 + j
            copy = send(
                prod.at[piece(chip * 2 + 1 - c, h)], core_in.at[chip, pl.ds(h * HALF, HALF)],
                core_s.at[base + j], core_r.at[base + j], mate,
            )
            copy.start()
            copies.append(copy)
        return copies

    def scatter(half, h, copies, prod, core_in, out, landing, own, base):
        at = pl.ds(h * HALF, HALF)
        for j in (0, 1):
            chip = half * 2 + j
            copies[j].wait_recv()
            both = prod[piece(chip * 2 + c, h)].astype(F32) + core_in[chip, at].astype(F32)

            @pl.when(chip == y)
            def _():
                own[at] = both

            @pl.when(chip != y)
            def _():
                k = (chip - y + NY) % NY - 1
                out[chip, at] = both.astype(BF16)
                send(
                    out.at[chip, at], landing.at[k, at],
                    ring_s.at[base + k], ring_r.at[base + k], (s, q, chip * 2 + c),
                ).start()

    def ring(k, h, out, landing, base):
        at = pl.ds(h * HALF, HALF)
        return send(
            out.at[0, at], landing.at[k, at],
            ring_s.at[base + k], ring_r.at[base + k], at_y(k + 1),
        )

    def collect(out, landing, own, base):
        value = own[...]
        for k in range(3):
            for h in (0, 1):
                ring(k, h, out, landing, base + 3 * h).wait_recv()
            value = value + landing[k].astype(F32)
        return value

    near_half, far_half = zh, 1 - zh

    def project_a(half, h, base):
        return project(half, h, tok_a, rot_v, False, prod_a, core_a, base)

    def project_u(half, h, base):
        return project(half, h, tok_u, quant, True, prod_u, core_u, base)

    def scatter_a(half, h, copies):
        scatter(half, h, copies, prod_a, core_a, send_a, recv_a, own_a, 3 * h)

    def scatter_u(half, h, copies):
        scatter(half, h, copies, prod_u, core_u, send_u, recv_u, own_u, 6 + 3 * h)

    def arrive(copies):
        for copy in copies:
            copy.wait_recv()

    follow(a_far[0], a_far[1])
    arrive(a_near)
    mates = [project_a(near_half, 0, 0), project_a(near_half, 1, 2)]
    follow(a_far[1], u_far[0])
    relay(a_far[0], a_pass[0])
    scatter_a(near_half, 0, mates[0])
    scatter_a(near_half, 1, mates[1])
    arrive(u_near)
    mates += [project_u(near_half, 0, 8), project_u(near_half, 1, 10)]
    arrive(a_pass[0])
    mates.append(project_a(far_half, 0, 4))
    relay(a_far[1], a_pass[1])
    follow(u_far[0], u_far[1])
    scatter_a(far_half, 0, mates[4])
    scatter_u(near_half, 0, mates[2])
    scatter_u(near_half, 1, mates[3])
    arrive(a_pass[1])
    mates.append(project_a(far_half, 1, 6))
    relay(u_far[0], u_pass[0])
    scatter_a(far_half, 1, mates[5])
    relay(u_far[1], u_pass[1])

    rotated = collect(send_a, recv_a, own_a, 0)
    own_a[...] = rotated
    peak = jnp.max(jnp.abs(rotated), axis=1, keepdims=True)
    diagonal = lax.broadcasted_iota(jnp.int32, (TOK, 128), 0) == lax.broadcasted_iota(
        jnp.int32, (TOK, 128), 1
    )
    line = jnp.max(jnp.where(diagonal, peak, 0.0), axis=0, keepdims=True)
    peak_own[...] = jnp.broadcast_to(line, (8, 128))
    peaks = [
        send(peak_own, peak_recv.at[i], peak_s.at[i], peak_r.at[i], device)
        for i, device in enumerate([at_x(k) for k in (1, 2, 3)] + [at_far(k) for k in range(4)])
    ]
    for copy in reversed(peaks):
        copy.start()
    for h in (0, 1):
        arrive(u_pass[h])
        mates.append(project_u(far_half, h, 12 + 2 * h))
        scatter_u(far_half, h, mates[-1])

    def turn(i, carry):
        r = pl.ds(pl.multiple_of(i * 128, 128), 128)
        acts_t[r] = tok_a[:, r].T
        return carry

    lax.fori_loop(0, WIDE // 128, turn, 0)
    for copy in peaks:
        copy.wait_recv()
    line = jnp.maximum(peak_own[...], jnp.max(peak_recv[...], axis=0))[0:1]
    peak = jnp.max(jnp.where(diagonal, line, 0.0), axis=1, keepdims=True)
    clip = ACT_CLIP * (peak + 1e-06)
    ratio = jnp.tanh(own_a[...] * (1.0 / clip))
    gate[...] = 1.0 - ratio * ratio

    def part(block, p):
        return grads.at[rows(block), pl.ds(*parts[p])]

    back = collect(send_u, recv_u, own_u, 6)
    g_y, g_core, g_pass = [], [], []
    for p in range(PARTS):
        at = pl.ds(*parts[p])
        grad = (back[:, p * PCOL : (p + 1) * PCOL] * gate[:, at]).astype(BF16)
        grads[rows(t), at] = grad
        base = 7 * p
        g_y.append([
            send(part(t, p), part(t, p), grad_s.at[base + k], grad_r.at[base + k], at_y(k))
            for k in (1, 2, 3)
        ])
        g_core.append(send(part(t, p), part(t, p), grad_s.at[base], grad_r.at[base], mate))
        for copy in g_y[p] + [g_core[p]]:
            copy.start()
        passing = []
        for k in (1, 2, 3):
            block = ((y - k + NY) % NY) * 2 + c
            i = base + 3 + k
            passing.append(send(part(block, p), part(block, p), grad_s.at[i], grad_r.at[i], mate))
        g_pass.append(passing)

    store_grad = pltpu.make_async_copy(grads.at[rows(t)], grad_out.at[0], local_sem.at[4])
    store_grad.start()

    def assemble(p):
        for arrived, onward in zip(g_y[p], g_pass[p]):
            arrived.wait_recv()
            onward.start()
        for copy in [g_core[p]] + g_pass[p]:
            copy.wait_recv()

    def partial(shard, p):
        return jnp.dot(
            acts_t[rows(shard, SHARD)], grads[:, p * PCOL : (p + 1) * PCOL],
            preferred_element_type=F32,
        )

    def hop(shard, p, out, landing, ssem, rsem, device):
        return send(
            out.at[shard, p], landing.at[shard, p], ssem.at[shard, p], rsem.at[shard, p], device
        )

    def step(tau, p):
        @pl.when(tau >= s)
        def _():
            shard = last - (tau - s)
            value = partial(shard, p)
            copy = hop(shard, p, right_send, right_recv, right_s, right_r, up)

            @pl.when(s > 0)
            def _():
                copy.wait_recv()
                right_send[shard, p] = (value + right_recv[shard, p].astype(F32)).astype(BF16)

            @pl.when(s == 0)
            def _():
                right_send[shard, p] = value.astype(BF16)

            copy.start()

        @pl.when(tau >= last - s)
        def _():
            shard = tau - (last - s)
            value = partial(shard, p)
            copy = hop(shard, p, left_send, left_recv, left_s, left_r, down)

            @pl.when(s < last)
            def _():
                copy.wait_recv()
                left_send[shard, p] = (value + left_recv[shard, p].astype(F32)).astype(BF16)

            @pl.when(s == last)
            def _():
                left_send[shard, p] = value.astype(BF16)

            copy.start()

    for p in range(PARTS):
        assemble(p)
        step(0, p)

    def steps(tau, carry):
        for p in range(PARTS):
            step(tau, p)
        return carry

    lax.fori_loop(1, last, steps, 0)
    stores = []
    for p in range(PARTS):
        cols = pl.ds(*parts[p])
        total[:, cols] = partial(s, p)

        @pl.when(s > 0)
        def _():
            hop(s, p, right_send, right_recv, right_s, right_r, up).wait_recv()
            total[:, cols] = total[:, cols] + right_recv[s, p].astype(F32)

        @pl.when(s < last)
        def _():
            hop(s, p, left_send, left_recv, left_s, left_r, down).wait_recv()
            total[:, cols] = total[:, cols] + left_recv[s, p].astype(F32)

        stores.append(pltpu.make_async_copy(total.at[:, cols], total_out.at[:, cols], local_sem.at[5 + p]))
        stores[p].start()

    for copy in a_pass[0] + a_pass[1] + u_near + u_far[1:] + u_pass[0] + u_pass[1]:
        copy.wait_send()

    @pl.when(s > 0)
    def _():
        u_shift.wait_send()

    for copy in a_near + sum(mates, peaks):
        copy.wait_send()
    for p in range(PARTS):
        for copy in g_y[p] + [g_core[p]] + g_pass[p]:
            copy.wait_send()
    for k in range(3):
        for h in (0, 1):
            ring(k, h, send_a, recv_a, 3 * h).wait_send()
            ring(k, h, send_u, recv_u, 6 + 3 * h).wait_send()

    def drain(shard, carry):
        for p in range(PARTS):

            @pl.when(shard > s)
            def _():
                hop(shard, p, right_send, right_recv, right_s, right_r, up).wait_send()

            @pl.when(shard < s)
            def _():
                hop(shard, p, left_send, left_recv, left_s, left_r, down).wait_send()

        return carry

    lax.fori_loop(0, n_sec, drain, 0)
    for store in [store_grad] + stores:
        store.wait()


def hand_on(total, grad, total_out, grad_out, total_v, grad_v, in_sem, out_sem):
    quarters = [pl.ds(i * (SHARD // 4), SHARD // 4) for i in range(4)]
    loads = [
        pltpu.make_async_copy(total.at[r], total_v.at[r], in_sem.at[i])
        for i, r in enumerate(quarters)
    ] + [pltpu.make_async_copy(grad, grad_v, in_sem.at[4])]
    stores = [
        pltpu.make_async_copy(total_v.at[r], total_out.at[r], out_sem.at[i])
        for i, r in enumerate(quarters)
    ] + [pltpu.make_async_copy(grad_v, grad_out, out_sem.at[4])]
    for load in loads:
        load.start()
    for load, store in zip(loads, stores):
        load.wait()
        store.start()
    for store in stores:
        store.wait()


def body(acts, incoming, rotation, q_weight, w_exponents):
    hbm = pl.BlockSpec(memory_space=pltpu.HBM)
    vmem = pl.BlockSpec(memory_space=pltpu.VMEM)
    dma = pltpu.SemaphoreType.DMA
    n_sec = lax.axis_size("section")
    hops = (n_sec, PARTS, SHARD, PCOL)
    total, grad = pl.pallas_call(
        kernel,
        name="rotation_gradient",
        out_shape=(
            jax.ShapeDtypeStruct((SHARD, WIDE), F32),
            jax.ShapeDtypeStruct((1, TOK, WIDE), BF16),
        ),
        in_specs=[hbm, hbm, hbm, hbm, vmem],
        out_specs=(hbm, hbm),
        scratch_shapes=[
            pltpu.VMEM((SHARD, WIDE), F32),
            pltpu.VMEM((8 * TOK, WIDE), BF16),
            pltpu.VMEM((8 * TOK, WIDE), BF16),
            pltpu.VMEM((WIDE, WIDE), BF16),
            pltpu.VMEM((WIDE, WIDE), BF16),
            pltpu.VMEM((WIDE, WIDE), BF16),
            pltpu.VMEM((WIDE, 8 * TOK), BF16),
            pltpu.VMEM((8 * TOK, WIDE), BF16),
            pltpu.VMEM((8 * TOK, WIDE), BF16),
            pltpu.VMEM((NY, TOK, WIDE), BF16),
            pltpu.VMEM((NY, TOK, WIDE), BF16),
            pltpu.VMEM((NY, TOK, WIDE), BF16),
            pltpu.VMEM((NY, TOK, WIDE), BF16),
            pltpu.VMEM((3, TOK, WIDE), BF16),
            pltpu.VMEM((3, TOK, WIDE), BF16),
            pltpu.VMEM((TOK, WIDE), F32),
            pltpu.VMEM((TOK, WIDE), F32),
            pltpu.VMEM((8, 128), F32),
            pltpu.VMEM((7, 8, 128), F32),
            pltpu.VMEM((TOK, WIDE), F32),
            pltpu.VMEM((8 * TOK, WIDE), BF16),
            pltpu.VMEM(hops, BF16),
            pltpu.VMEM(hops, BF16),
            pltpu.VMEM(hops, BF16),
            pltpu.VMEM(hops, BF16),
            dma((5 + PARTS,)),
            dma((11,)), dma((11,)), dma((12,)), dma((12,)),
            dma((16,)), dma((16,)), dma((12,)), dma((12,)),
            dma((7,)), dma((7,)), dma((7 * PARTS,)), dma((7 * PARTS,)),
            dma((n_sec, PARTS)), dma((n_sec, PARTS)),
            dma((n_sec, PARTS)), dma((n_sec, PARTS)),
        ],
        compiler_params=pltpu.CompilerParams(
            collective_id=0, has_side_effects=True, vmem_limit_bytes=VMEM_LIMIT
        ),
        cost_estimate=pl.CostEstimate(
            flops=3 * 2 * 512 * WIDE * WIDE, bytes_accessed=6 * 2**20, transcendentals=2**20
        ),
    )(acts, incoming, rotation, q_weight, w_exponents)
    return pl.pallas_call(
        hand_on,
        name="results",
        out_shape=(
            jax.ShapeDtypeStruct((SHARD, WIDE), F32),
            jax.ShapeDtypeStruct((1, TOK, WIDE), BF16),
        ),
        in_specs=[hbm, hbm],
        out_specs=(hbm, hbm),
        scratch_shapes=[
            pltpu.VMEM((SHARD, WIDE), F32),
            pltpu.VMEM((1, TOK, WIDE), BF16),
            dma((5,)), dma((5,)),
        ],
        compiler_params=pltpu.CompilerParams(vmem_limit_bytes=VMEM_LIMIT),
    )(total, grad)


def solution(mesh):
    placed = (
        P("section", "seq", "tensor"),
        P("section", "seq", "tensor"),
        P("tensor", "seq"),
        P("section", "seq", "tensor"),
        P("section", "tensor"),
    )
    return jax.shard_map(
        body,
        mesh=mesh,
        in_specs=placed,
        out_specs=(P(("tensor", "section"), "seq"), P("section", "tensor", "seq")),
        check_vma=False,
    )
```

```python
import jax
import jax.numpy as jnp
from jax import lax
from jax.experimental import pallas as pl
from jax.experimental.pallas import tpu as pltpu
from jax.sharding import PartitionSpec as P

F32, BF16 = jnp.float32, jnp.bfloat16
ACT_CLIP = 0.5
VMEM_LIMIT = 63 * 2**20
NX, NY = 4, 4
TOK = 64
WIDE = 1024
SHARD = 128
PARTS = 8
PCOL = WIDE // PARTS
TILE = 256
HALF = TOK // 2


def kernel(
    acts, incoming, rotation, weight, expos,
    total_out, grad_out,
    total, tok_a, tok_u, rot_v, w_v, quant, acts_t,
    prod_a, prod_u, core_a, core_u, send_a, send_u, recv_a, recv_u,
    own_a, own_u, peak_own, peak_recv, gate, grads,
    right_send, right_recv, left_send, left_recv,
    local_sem, gather_a_s, gather_a_r, gather_u_s, gather_u_r,
    core_s, core_r, ring_s, ring_r, peak_s, peak_r, grad_s, grad_r,
    right_s, right_r, left_s, left_r,
):
    n_sec = lax.axis_size("section")
    s = lax.axis_index("section")
    q = lax.axis_index("seq")
    t = lax.axis_index("tensor")
    zh, x = q // NX, q % NX
    y, c = t // 2, t % 2
    last = n_sec - 1

    def at_x(k):
        return (s, zh * NX + (x + k) % NX, t)

    def at_y(k):
        return (s, q, ((y + k) % NY) * 2 + c)

    def at_far(k):
        return (s, (1 - zh) * NX + (x + k) % NX, t)

    far = at_far(0)
    mate = (s, q, y * 2 + 1 - c)
    up, down = (s + 1, q, t), (s - 1, q, t)

    def signal(device):
        pl.semaphore_signal(barrier, inc=1, device_id=device, device_id_type=pl.DeviceIdType.MESH)

    def send(src, dst, ssem, rsem, device):
        return pltpu.make_async_remote_copy(
            src_ref=src, dst_ref=dst, send_sem=ssem, recv_sem=rsem,
            device_id=device, device_id_type=pl.DeviceIdType.MESH,
        )

    def rows(block, size=TOK):
        return pl.ds(pl.multiple_of(block * size, size), size)

    load_rot = pltpu.make_async_copy(rotation, rot_v, local_sem.at[0])
    load_w = pltpu.make_async_copy(weight.at[0], w_v, local_sem.at[1])
    load_a = pltpu.make_async_copy(acts.at[0], tok_a.at[rows(q)], local_sem.at[2])
    load_u = pltpu.make_async_copy(incoming.at[0], tok_u.at[rows(q)], local_sem.at[3])
    load_a.start()
    load_w.start()
    load_rot.start()

    @pl.when(s == last)
    def _():
        load_u.start()

    barrier = pltpu.get_barrier_semaphore()
    for k in (1, 2, 3):
        signal(at_x(k))
        signal(at_y(k))
    for k in range(4):
        signal(at_far(k))
    signal(mate)

    @pl.when(s < last)
    def _():
        signal(up)

    @pl.when(s > 0)
    def _():
        signal(down)

    load_w.wait()
    scale = 127.0 * jnp.exp2(expos[...].astype(F32))
    inverse = 1.0 / scale

    def quantize(i, carry):
        r = rows(i, 64)
        quant[r] = (scale * jnp.tanh(w_v[r].astype(F32) * inverse)).astype(BF16)
        return carry

    lax.fori_loop(0, WIDE // 64, quantize, 0)
    pl.semaphore_wait(
        barrier, 11 + jnp.where(s < last, 1, 0) + jnp.where(s > 0, 1, 0)
    )

    mine = rows(q)

    def piece(block, h):
        return pl.ds(pl.multiple_of(block * TOK + h * HALF, HALF), HALF)

    def gather(first, tok, ssem, rsem):
        other = (1 - zh) * NX + x
        near = [
            send(first, tok.at[mine], ssem.at[k - 1], rsem.at[k - 1], at_x(k)) for k in (1, 2, 3)
        ]
        across = [
            send(
                first.at[pl.ds(h * HALF, HALF)], tok.at[piece(q, h)],
                ssem.at[3 + h], rsem.at[3 + h], far,
            )
            for h in (0, 1)
        ]
        onward = [
            [
                send(
                    tok.at[piece(other, h)], tok.at[piece(other, h)],
                    ssem.at[4 + 3 * h + k], rsem.at[4 + 3 * h + k], at_x(k),
                )
                for k in (1, 2, 3)
            ]
            for h in (0, 1)
        ]
        return near, across, onward

    a_near, a_far, a_pass = gather(acts.at[0], tok_a, gather_a_s, gather_a_r)
    u_near, u_far, u_pass = gather(tok_u.at[mine], tok_u, gather_u_s, gather_u_r)
    u_shift = send(incoming.at[0], tok_u.at[mine], gather_u_s.at[11], gather_u_r.at[11], down)

    def relay(arriving, onward):
        arriving.wait_recv()
        for copy in onward:
            copy.start()

    @pl.when(s > 0)
    def _():
        u_shift.start()

    a_far[0].start()
    for copy in a_near:
        copy.start()

    @pl.when(s < last)
    def _():
        u_shift.wait_recv()

    @pl.when(s == last)
    def _():
        load_u.wait()

    for copy in u_near:
        copy.start()

    load_rot.wait()
    load_a.wait()

    def follow(done, copy):
        done.wait_send()
        copy.start()

    parts = [(p * PCOL, PCOL) for p in range(PARTS)]

    def project(half, h, tok, mat, flip, prod, core_in, base):
        value = jnp.concatenate([tok[piece(half * NX + i, h)] for i in range(NX)], axis=0)

        def tile(n, carry):
            at = pl.ds(pl.multiple_of(n * TILE, TILE), TILE)
            if flip:
                result = lax.dot_general(
                    value, mat[at], (((1,), (1,)), ((), ())), preferred_element_type=F32
                )
            else:
                result = jnp.dot(value, mat[:, at], preferred_element_type=F32)
            for i in range(NX):
                prod[piece(half * NX + i, h), at] = result[i * HALF : (i + 1) * HALF].astype(BF16)
            return carry

        lax.fori_loop(0, WIDE // TILE, tile, 0)
        copies = []
        for j in (0, 1):
            chip = half * 2 + j
            copy = send(
                prod.at[piece(chip * 2 + 1 - c, h)], core_in.at[chip, pl.ds(h * HALF, HALF)],
                core_s.at[base + j], core_r.at[base + j], mate,
            )
            copy.start()
            copies.append(copy)
        return copies

    def scatter(half, h, copies, prod, core_in, out, landing, own, base):
        at = pl.ds(h * HALF, HALF)
        for j in (0, 1):
            chip = half * 2 + j
            copies[j].wait_recv()
            both = prod[piece(chip * 2 + c, h)].astype(F32) + core_in[chip, at].astype(F32)

            @pl.when(chip == y)
            def _():
                own[at] = both

            @pl.when(chip != y)
            def _():
                k = (chip - y + NY) % NY - 1
                out[chip, at] = both.astype(BF16)
                send(
                    out.at[chip, at], landing.at[k, at],
                    ring_s.at[base + k], ring_r.at[base + k], (s, q, chip * 2 + c),
                ).start()

    def ring(k, h, out, landing, base):
        at = pl.ds(h * HALF, HALF)
        return send(
            out.at[0, at], landing.at[k, at],
            ring_s.at[base + k], ring_r.at[base + k], at_y(k + 1),
        )

    def collect(out, landing, own, base):
        value = own[...]
        for k in range(3):
            for h in (0, 1):
                ring(k, h, out, landing, base + 3 * h).wait_recv()
            value = value + landing[k].astype(F32)
        return value

    near_half, far_half = zh, 1 - zh

    def project_a(half, h, base):
        return project(half, h, tok_a, rot_v, False, prod_a, core_a, base)

    def project_u(half, h, base):
        return project(half, h, tok_u, quant, True, prod_u, core_u, base)

    def scatter_a(half, h, copies):
        scatter(half, h, copies, prod_a, core_a, send_a, recv_a, own_a, 3 * h)

    def scatter_u(half, h, copies):
        scatter(half, h, copies, prod_u, core_u, send_u, recv_u, own_u, 6 + 3 * h)

    def arrive(copies):
        for copy in copies:
            copy.wait_recv()

    follow(a_far[0], a_far[1])
    arrive(a_near)
    mates = [project_a(near_half, 0, 0), project_a(near_half, 1, 2)]
    follow(a_far[1], u_far[0])
    relay(a_far[0], a_pass[0])
    scatter_a(near_half, 0, mates[0])
    scatter_a(near_half, 1, mates[1])
    arrive(u_near)
    mates += [project_u(near_half, 0, 8), project_u(near_half, 1, 10)]
    arrive(a_pass[0])
    mates.append(project_a(far_half, 0, 4))
    relay(a_far[1], a_pass[1])
    follow(u_far[0], u_far[1])
    scatter_a(far_half, 0, mates[4])
    scatter_u(near_half, 0, mates[2])
    scatter_u(near_half, 1, mates[3])
    arrive(a_pass[1])
    mates.append(project_a(far_half, 1, 6))
    relay(u_far[0], u_pass[0])
    scatter_a(far_half, 1, mates[5])
    relay(u_far[1], u_pass[1])

    rotated = collect(send_a, recv_a, own_a, 0)
    own_a[...] = rotated
    peak = jnp.max(jnp.abs(rotated), axis=1, keepdims=True)
    diagonal = lax.broadcasted_iota(jnp.int32, (TOK, 128), 0) == lax.broadcasted_iota(
        jnp.int32, (TOK, 128), 1
    )
    line = jnp.max(jnp.where(diagonal, peak, 0.0), axis=0, keepdims=True)
    peak_own[...] = jnp.broadcast_to(line, (8, 128))
    peaks = [
        send(peak_own, peak_recv.at[i], peak_s.at[i], peak_r.at[i], device)
        for i, device in enumerate([at_x(k) for k in (1, 2, 3)] + [at_far(k) for k in range(4)])
    ]
    for copy in reversed(peaks):
        copy.start()
    for h in (0, 1):
        arrive(u_pass[h])
        mates.append(project_u(far_half, h, 12 + 2 * h))
        scatter_u(far_half, h, mates[-1])

    def turn(i, carry):
        r = pl.ds(pl.multiple_of(i * 128, 128), 128)
        acts_t[r] = tok_a[:, r].T
        return carry

    lax.fori_loop(0, WIDE // 128, turn, 0)
    for copy in peaks:
        copy.wait_recv()
    line = jnp.maximum(peak_own[...], jnp.max(peak_recv[...], axis=0))[0:1]
    peak = jnp.max(jnp.where(diagonal, line, 0.0), axis=1, keepdims=True)
    clip = ACT_CLIP * (peak + 1e-06)
    ratio = jnp.tanh(own_a[...] * (1.0 / clip))
    gate[...] = 1.0 - ratio * ratio

    def part(block, p):
        return grads.at[rows(block), pl.ds(*parts[p])]

    back = collect(send_u, recv_u, own_u, 6)
    g_y, g_core, g_pass = [], [], []
    for p in range(PARTS):
        at = pl.ds(*parts[p])
        grad = (back[:, p * PCOL : (p + 1) * PCOL] * gate[:, at]).astype(BF16)
        grads[rows(t), at] = grad
        base = 7 * p
        g_y.append([
            send(part(t, p), part(t, p), grad_s.at[base + k], grad_r.at[base + k], at_y(k))
            for k in (1, 2, 3)
        ])
        g_core.append(send(part(t, p), part(t, p), grad_s.at[base], grad_r.at[base], mate))
        for copy in g_y[p] + [g_core[p]]:
            copy.start()
        passing = []
        for k in (1, 2, 3):
            block = ((y - k + NY) % NY) * 2 + c
            i = base + 3 + k
            passing.append(send(part(block, p), part(block, p), grad_s.at[i], grad_r.at[i], mate))
        g_pass.append(passing)

    store_grad = pltpu.make_async_copy(grads.at[rows(t)], grad_out.at[0], local_sem.at[4])
    store_grad.start()

    def assemble(p):
        for arrived, onward in zip(g_y[p], g_pass[p]):
            arrived.wait_recv()
            onward.start()
        for copy in [g_core[p]] + g_pass[p]:
            copy.wait_recv()

    def partial(shard, p):
        return jnp.dot(
            acts_t[rows(shard, SHARD)], grads[:, p * PCOL : (p + 1) * PCOL],
            preferred_element_type=F32,
        )

    def hop(shard, p, out, landing, ssem, rsem, device):
        return send(
            out.at[shard, p], landing.at[shard, p], ssem.at[shard, p], rsem.at[shard, p], device
        )

    def step(tau, p):
        @pl.when(tau >= s)
        def _():
            shard = last - (tau - s)
            value = partial(shard, p)
            copy = hop(shard, p, right_send, right_recv, right_s, right_r, up)

            @pl.when(s > 0)
            def _():
                copy.wait_recv()
                right_send[shard, p] = (value + right_recv[shard, p].astype(F32)).astype(BF16)

            @pl.when(s == 0)
            def _():
                right_send[shard, p] = value.astype(BF16)

            copy.start()

        @pl.when(tau >= last - s)
        def _():
            shard = tau - (last - s)
            value = partial(shard, p)
            copy = hop(shard, p, left_send, left_recv, left_s, left_r, down)

            @pl.when(s < last)
            def _():
                copy.wait_recv()
                left_send[shard, p] = (value + left_recv[shard, p].astype(F32)).astype(BF16)

            @pl.when(s == last)
            def _():
                left_send[shard, p] = value.astype(BF16)

            copy.start()

    for p in range(PARTS):
        assemble(p)
        step(0, p)

    def steps(tau, carry):
        for p in range(PARTS):
            step(tau, p)
        return carry

    lax.fori_loop(1, last, steps, 0)
    stores = []
    for p in range(PARTS):
        cols = pl.ds(*parts[p])
        total[:, cols] = partial(s, p)

        @pl.when(s > 0)
        def _():
            hop(s, p, right_send, right_recv, right_s, right_r, up).wait_recv()
            total[:, cols] = total[:, cols] + right_recv[s, p].astype(F32)

        @pl.when(s < last)
        def _():
            hop(s, p, left_send, left_recv, left_s, left_r, down).wait_recv()
            total[:, cols] = total[:, cols] + left_recv[s, p].astype(F32)

        stores.append(pltpu.make_async_copy(total.at[:, cols], total_out.at[:, cols], local_sem.at[5 + p]))
        stores[p].start()

    for copy in a_pass[0] + a_pass[1] + u_near + u_far[1:] + u_pass[0] + u_pass[1]:
        copy.wait_send()

    @pl.when(s > 0)
    def _():
        u_shift.wait_send()

    for copy in a_near + sum(mates, peaks):
        copy.wait_send()
    for p in range(PARTS):
        for copy in g_y[p] + [g_core[p]] + g_pass[p]:
            copy.wait_send()
    for k in range(3):
        for h in (0, 1):
            ring(k, h, send_a, recv_a, 3 * h).wait_send()
            ring(k, h, send_u, recv_u, 6 + 3 * h).wait_send()

    def drain(shard, carry):
        for p in range(PARTS):

            @pl.when(shard > s)
            def _():
                hop(shard, p, right_send, right_recv, right_s, right_r, up).wait_send()

            @pl.when(shard < s)
            def _():
                hop(shard, p, left_send, left_recv, left_s, left_r, down).wait_send()

        return carry

    lax.fori_loop(0, n_sec, drain, 0)
    for store in [store_grad] + stores:
        store.wait()


def hand_on(total, grad, total_out, grad_out, total_v, grad_v, in_sem, out_sem):
    quarters = [pl.ds(i * (SHARD // 4), SHARD // 4) for i in range(4)]
    loads = [
        pltpu.make_async_copy(total.at[r], total_v.at[r], in_sem.at[i])
        for i, r in enumerate(quarters)
    ] + [pltpu.make_async_copy(grad, grad_v, in_sem.at[4])]
    stores = [
        pltpu.make_async_copy(total_v.at[r], total_out.at[r], out_sem.at[i])
        for i, r in enumerate(quarters)
    ] + [pltpu.make_async_copy(grad_v, grad_out, out_sem.at[4])]
    for load in loads:
        load.start()
    for load, store in zip(loads, stores):
        load.wait()
        store.start()
    for store in stores:
        store.wait()


def body(acts, incoming, rotation, q_weight, w_exponents):
    hbm = pl.BlockSpec(memory_space=pltpu.HBM)
    vmem = pl.BlockSpec(memory_space=pltpu.VMEM)
    dma = pltpu.SemaphoreType.DMA
    n_sec = lax.axis_size("section")
    hops = (n_sec, PARTS, SHARD, PCOL)
    total, grad = pl.pallas_call(
        kernel,
        name="rotation_gradient",
        out_shape=(
            jax.ShapeDtypeStruct((SHARD, WIDE), F32),
            jax.ShapeDtypeStruct((1, TOK, WIDE), BF16),
        ),
        in_specs=[hbm, hbm, hbm, hbm, vmem],
        out_specs=(hbm, hbm),
        scratch_shapes=[
            pltpu.VMEM((SHARD, WIDE), F32),
            pltpu.VMEM((8 * TOK, WIDE), BF16),
            pltpu.VMEM((8 * TOK, WIDE), BF16),
            pltpu.VMEM((WIDE, WIDE), BF16),
            pltpu.VMEM((WIDE, WIDE), BF16),
            pltpu.VMEM((WIDE, WIDE), BF16),
            pltpu.VMEM((WIDE, 8 * TOK), BF16),
            pltpu.VMEM((8 * TOK, WIDE), BF16),
            pltpu.VMEM((8 * TOK, WIDE), BF16),
            pltpu.VMEM((NY, TOK, WIDE), BF16),
            pltpu.VMEM((NY, TOK, WIDE), BF16),
            pltpu.VMEM((NY, TOK, WIDE), BF16),
            pltpu.VMEM((NY, TOK, WIDE), BF16),
            pltpu.VMEM((3, TOK, WIDE), BF16),
            pltpu.VMEM((3, TOK, WIDE), BF16),
            pltpu.VMEM((TOK, WIDE), F32),
            pltpu.VMEM((TOK, WIDE), F32),
            pltpu.VMEM((8, 128), F32),
            pltpu.VMEM((7, 8, 128), F32),
            pltpu.VMEM((TOK, WIDE), F32),
            pltpu.VMEM((8 * TOK, WIDE), BF16),
            pltpu.VMEM(hops, BF16),
            pltpu.VMEM(hops, BF16),
            pltpu.VMEM(hops, BF16),
            pltpu.VMEM(hops, BF16),
            dma((5 + PARTS,)),
            dma((11,)), dma((11,)), dma((12,)), dma((12,)),
            dma((16,)), dma((16,)), dma((12,)), dma((12,)),
            dma((7,)), dma((7,)), dma((7 * PARTS,)), dma((7 * PARTS,)),
            dma((n_sec, PARTS)), dma((n_sec, PARTS)),
            dma((n_sec, PARTS)), dma((n_sec, PARTS)),
        ],
        compiler_params=pltpu.CompilerParams(
            collective_id=0, has_side_effects=True, vmem_limit_bytes=VMEM_LIMIT
        ),
        cost_estimate=pl.CostEstimate(
            flops=3 * 2 * 512 * WIDE * WIDE, bytes_accessed=6 * 2**20, transcendentals=2**20
        ),
    )(acts, incoming, rotation, q_weight, w_exponents)
    return pl.pallas_call(
        hand_on,
        name="results",
        out_shape=(
            jax.ShapeDtypeStruct((SHARD, WIDE), F32),
            jax.ShapeDtypeStruct((1, TOK, WIDE), BF16),
        ),
        in_specs=[hbm, hbm],
        out_specs=(hbm, hbm),
        scratch_shapes=[
            pltpu.VMEM((SHARD, WIDE), F32),
            pltpu.VMEM((1, TOK, WIDE), BF16),
            dma((5,)), dma((5,)),
        ],
        compiler_params=pltpu.CompilerParams(vmem_limit_bytes=VMEM_LIMIT),
    )(total, grad)


def solution(mesh):
    placed = (
        P("section", "seq", "tensor"),
        P("section", "seq", "tensor"),
        P("tensor", "seq"),
        P("section", "seq", "tensor"),
        P("section", "tensor"),
    )
    return jax.shard_map(
        body,
        mesh=mesh,
        in_specs=placed,
        out_specs=(P(("tensor", "section"), "seq"), P("section", "tensor", "seq")),
        check_vma=False,
    )
```
